32 devices in a mesh: dp: 8 (over y, x, core), expert: 4 (over z).
Axes of the slice: x: 2, y: 2, z: 4, core: 2. Of those that a mesh axis runs over, the one named last changes fastest.
Arguments:
- tokens: bfloat16 [512, 4096], P('expert', 'dp'), may hold values from -6 to 6
- expert_ids: int32 [512, 8], P('expert'), may hold values from 0 to 15, all different within a row; in each aligned block of 128 rows (0 to 127, 128 to 255, ...) at most 128 rows name the same one
- gate_prob: float32 [512, 8], P('expert'), may hold values from 0.05 to 0.35
- w_gate: bfloat16 [16, 4096, 768], P('expert', 'dp'), may hold values from -0.09375 to 0.09375
- w_up: bfloat16 [16, 4096, 768], P('expert', 'dp'), may hold values from -0.09375 to 0.09375
- w_down: bfloat16 [16, 768, 4096], P('expert', None, 'dp'), may hold values from -0.21875 to 0.21875
- grad_out: bfloat16 [512, 4096], P('expert', 'dp'), may hold values from -6 to 6
Outputs:
- mixed: bfloat16 [512, 4096], P('expert', 'dp')
- grad_tokens: bfloat16 [512, 4096], P('expert', 'dp')
- grad_gate: float32 [512, 8], P('expert')
- grad_w_gate: bfloat16 [16, 4096, 768], P('expert', 'dp')
- grad_w_up: bfloat16 [16, 4096, 768], P('expert', 'dp')
- grad_w_down: bfloat16 [16, 768, 4096], P('expert', None, 'dp')
The draws below stay inside these ranges and needn't reach their ends.
Inputs may be any that keep to these rules, and one draw needn't show every extreme that they name: `expert_ids`: each row names 8 different experts. Within the rows of one index of expert (aligned blocks of 128 rows) no expert is named by more than 128 rows, a bound that some block reaches.
All inputs are finite; a program needn't handle non-finite values.
Results may differ from the reference program's by a relative error of at most 0.035.
Values may be sent and summed in bfloat16 or wider, within the bound.
A program may use at most 128 MiB of HBM per device.

```python
import math
import jax
import jax.numpy as jnp
import numpy as np
from jax import lax

D = 4096
FF = 768
TOPK = 8
TOK_COL = 128
EXPERTS = 16
TOKENS = 512
CAP = 128
N_DP = 8
N_EXPERT = 4


def block_scale(own_key, extent, shards, least, largest):
    def one(axis_at, blocks):
        draws = jax.random.uniform(jax.random.fold_in(jax.random.fold_in(own_key, 6), axis_at), (blocks,), jnp.float32, least / len(shards), largest / len(shards))
        return jnp.repeat(jnp.exp(draws), extent[axis_at] // blocks).reshape((-1,) + (1,) * (len(extent) - axis_at - 1))

    level = one(*shards[0])
    for cut in shards[1:]:
        level = level * one(*cut)
    return level


def routed_block(own_key, own, number, rows, number_of, top, most, slope):
    sequence = jax.random.permutation(own_key, number_of)
    heavy_load, common = shares(number_of, rows * top, most, slope, True), shares(number_of, rows * top, most, slope, False)
    places = jnp.arange(number_of)

    def named(tallies, rotation):
        used = int((tallies > 0).sum())
        fixed = max(1, used // 4)
        shifted = fixed + (places - fixed + rotation * (used - fixed)) % max(1, number_of - fixed)
        return jnp.zeros((number_of,), jnp.int32).at[sequence[jnp.where(places < fixed, places, shifted)]].set(jnp.asarray(tallies, jnp.int32))

    tallies = jnp.where(number % 4 == 0, named(heavy_load, number // 4), named(common, number - number // 4 - 1))
    mixed = jax.random.permutation(jax.random.fold_in(own, 3), number_of)
    donor, taker = mixed[0:number_of // 2 * 2:2], mixed[1:number_of // 2 * 2:2]
    margin = jnp.minimum(tallies[donor] - 1, most - tallies[taker]) // 2
    margin = jnp.where((donor == sequence[0]) | (taker == sequence[0]) | (tallies[taker] == 0), 0, jnp.maximum(margin, 0))
    shifted = jax.random.randint(jax.random.fold_in(own, 4), (number_of // 2,), 0, 1 << 20) % (margin + 1)
    tallies = tallies.at[donor].add(-shifted).at[taker].add(shifted)
    labels = jnp.searchsorted(jnp.cumsum(tallies), jnp.arange(rows * top), side="right").astype(jnp.int32)
    grid = labels.reshape(top, rows).T
    grid = grid[jax.random.permutation(jax.random.fold_in(own, 1), rows)]
    rotation = jax.random.randint(jax.random.fold_in(own, 2), (rows, 1), 0, top)
    return jnp.take_along_axis(grid, (jnp.arange(top)[None, :] + rotation) % top, axis=1)


def shares(amount, total, limit, lean, full):
    loads = [(1 << 20) // math.isqrt(grade ** lean) + 1 for grade in range(1, amount + 1)]
    largest = limit if full else min(limit, max(-(-total // amount), total * loads[0] // sum(loads)))
    least = 1 if total - largest >= amount - 1 else 0
    counts, rest = [largest] + [least] * (amount - 1), total - largest - least * (amount - 1)
    while rest > 0:
        movable = [i for i in range(1, amount) if counts[i] < largest] or [i for i in range(1, amount) if counts[i] < limit]
        whole, remaining = sum([loads[i] for i in movable]), rest
        for i in movable:
            extra = min(limit - counts[i], max(1, remaining * loads[i] // whole), rest)
            counts[i] = counts[i] + extra
            rest = rest - extra
    return np.array(counts)


def scatter_about(key, dims, width, reach, cuts=(), kind=jnp.bfloat16):
    values = jax.random.normal(key, dims, jnp.float32) * width
    if len(cuts) > 0:
        values = block_scale(key, dims, cuts, -0.22, 0.18) * values
    return jnp.clip(values, min=-reach, max=reach).astype(kind)


def setup_inputs(seed: int = 0) -> dict:
    streams_of = jax.random.split(jax.random.key(seed), 8)
    tokens = scatter_about(streams_of[0], (TOKENS, D), 1.0, 6.0, ((0, 4), (1, 8)))
    expert_ids_keys = jax.random.split(jax.random.fold_in(streams_of[1], 1), TOKENS // TOK_COL)
    expert_ids_turns = jax.random.permutation(jax.random.fold_in(streams_of[1], 3), TOKENS // TOK_COL)
    expert_ids = jax.vmap(lambda own, number: routed_block(jax.random.fold_in(streams_of[1], 2), own, number, TOK_COL, EXPERTS, TOPK, CAP, 2))(expert_ids_keys, expert_ids_turns).reshape((TOKENS, TOPK))
    gate_prob = jnp.clip(0.05 + 0.29999999 * jax.random.uniform(streams_of[2], (TOKENS, TOPK), jnp.float32) ** block_scale(streams_of[2], (TOKENS, TOPK), ((0, 4),), -0.2, 0.2), 0.05, 0.35)
    w_gate = scatter_about(streams_of[3], (EXPERTS, D, FF), D ** -0.5, 0.09375, ((0, 4), (1, 8)))
    w_up = scatter_about(streams_of[4], (EXPERTS, D, FF), D ** -0.5, 0.09375, ((0, 4), (1, 8)))
    w_down = scatter_about(streams_of[5], (EXPERTS, FF, D), FF ** -0.5, 0.21875, ((0, 4), (2, 8)))
    grad_out = scatter_about(streams_of[6], (TOKENS, D), 1.0, 6.0, ((0, 4), (1, 8)))
    return {"tokens": tokens, "expert_ids": expert_ids, "gate_prob": gate_prob, "w_gate": w_gate, "w_up": w_up, "w_down": w_down, "grad_out": grad_out}


def sliced_sum(row_slices, weight_slices):
    parts = jnp.einsum("mrd,rdf->rmf", row_slices.astype(jnp.float32), weight_slices.astype(jnp.float32))
    rounded = lax.optimization_barrier(parts.astype(jnp.bfloat16))
    return jnp.sum(rounded.astype(jnp.float32), axis=0)


def reference(tokens, expert_ids, gate_prob, w_gate, w_up, w_down, grad_out):
    tok_count = tokens.shape[0]
    flat_ids = expert_ids.reshape(-1).astype(jnp.int32)
    assign_count = flat_ids.shape[0]
    most_rows = N_EXPERT * CAP
    slice_width = D // N_DP
    gate_flat = gate_prob.reshape(-1)
    positions = jnp.arange(most_rows, dtype=jnp.int32)

    def per_expert(carry, expert):
        mixed_acc, grad_acc, gate_acc = carry
        chosen = flat_ids == expert
        picked = jnp.nonzero(chosen, size=most_rows, fill_value=0)[0].astype(jnp.int32)
        filled = positions < jnp.sum(chosen.astype(jnp.int32))
        tok_idx = picked // TOPK
        x_rows = jnp.where(filled[:, None], tokens[tok_idx], jnp.zeros((), jnp.bfloat16))
        dy_rows = grad_out[tok_idx].astype(jnp.float32)
        gates = jnp.where(filled, gate_flat[picked], jnp.zeros((), jnp.float32))
        scaled_grad = (gates[:, None] * dy_rows).astype(jnp.bfloat16)
        wg = w_gate[expert]
        wu = w_up[expert]
        wd = w_down[expert]
        x_slices = x_rows.reshape(most_rows, N_DP, slice_width)
        gate_pre = sliced_sum(x_slices, wg.reshape(N_DP, slice_width, FF))
        up_pre = sliced_sum(x_slices, wu.reshape(N_DP, slice_width, FF))
        hidden = (jax.nn.silu(gate_pre) * up_pre).astype(jnp.bfloat16)
        expert_out = jnp.dot(hidden, wd, preferred_element_type=jnp.float32).astype(jnp.bfloat16)
        grad_slices = scaled_grad.reshape(most_rows, N_DP, slice_width)
        down_slices = jnp.transpose(wd.reshape(FF, N_DP, slice_width), (1, 2, 0))
        hidden_grad = sliced_sum(grad_slices, down_slices)
        sigmoid_g = jax.nn.sigmoid(gate_pre)
        gate_grad = (hidden_grad * up_pre * sigmoid_g * (1.0 + gate_pre * (1.0 - sigmoid_g))).astype(jnp.bfloat16)
        up_grad = (hidden_grad * gate_pre * sigmoid_g).astype(jnp.bfloat16)
        token_part = (jnp.dot(gate_grad, wg.T, preferred_element_type=jnp.float32)
                      + jnp.dot(up_grad, wu.T, preferred_element_type=jnp.float32)).astype(jnp.bfloat16)
        dw_gate = jnp.dot(x_rows.T, gate_grad, preferred_element_type=jnp.float32).astype(jnp.bfloat16)
        dw_up = jnp.dot(x_rows.T, up_grad, preferred_element_type=jnp.float32).astype(jnp.bfloat16)
        dw_down = jnp.dot(hidden.T, scaled_grad, preferred_element_type=jnp.float32).astype(jnp.bfloat16)
        out_float = expert_out.astype(jnp.float32)
        mixed_acc = mixed_acc.at[tok_idx].add(gates[:, None] * out_float)
        grad_acc = grad_acc.at[tok_idx].add(jnp.where(filled[:, None], token_part.astype(jnp.float32), jnp.zeros((), jnp.float32)))
        dots = jnp.sum(out_float * dy_rows, axis=1)
        gate_acc = gate_acc.at[picked].add(jnp.where(filled, dots, jnp.zeros((), jnp.float32)))
        return (mixed_acc, grad_acc, gate_acc), (dw_gate, dw_up, dw_down)

    start = (jnp.zeros((tok_count, D), jnp.float32), jnp.zeros((tok_count, D), jnp.float32),
             jnp.zeros((assign_count,), jnp.float32))
    final, stacked = lax.scan(per_expert, start, jnp.arange(EXPERTS, dtype=jnp.int32))
    mixed_acc, grad_acc, gate_acc = final
    grad_w_gate, grad_w_up, grad_w_down = stacked
    mixed = mixed_acc.astype(jnp.bfloat16)
    grad_tokens = grad_acc.astype(jnp.bfloat16)
    grad_gate = gate_acc.reshape(tok_count, TOPK)
    return mixed, grad_tokens, grad_gate, grad_w_gate, grad_w_up, grad_w_down
```

```python
import jax
import jax.numpy as jnp
from jax import lax
from jax.sharding import PartitionSpec as P


def split_bf16(value):
    high = value.astype(jnp.bfloat16)
    rest = value - high.astype(jnp.float32)
    mid = rest.astype(jnp.bfloat16)
    low = (rest - mid.astype(jnp.float32)).astype(jnp.bfloat16)
    return high, mid, low


def exchange(x_rows, g_rows, probs, w_gate, w_up, w_down):
    per_device, rows, _ = probs.shape
    hidden_units = w_gate.shape[2]
    experts = range(per_device)
    scaled = (probs * g_rows.astype(jnp.float32)).astype(jnp.bfloat16)

    def dot(spec, a, b):
        return jnp.einsum(spec, a, b, preferred_element_type=jnp.float32).astype(jnp.bfloat16)

    x_all = jnp.broadcast_to(x_rows, (per_device,) + x_rows.shape[1:])
    part = jnp.concatenate(
        [
            dot("grd,gdf->grf", x_all, w_gate),
            dot("grd,gdf->grf", x_all, w_up),
            dot("grd,gfd->grf", scaled, w_down),
        ],
        axis=2,
    ).reshape(per_device * rows, 3 * hidden_units)
    share = lax.psum_scatter(part, "dp", scatter_dimension=0, tiled=True).astype(jnp.float32)
    gate, up, hgrad = jnp.split(share, 3, axis=1)
    sig = jax.nn.sigmoid(gate)
    act = jnp.concatenate(
        [gate * sig * up, hgrad * up * sig * (1.0 + gate * (1.0 - sig)), hgrad * gate * sig],
        axis=1,
    ).astype(jnp.bfloat16)
    full = lax.all_gather(act, "dp", axis=0, tiled=True).reshape(per_device, rows, 3 * hidden_units)
    return scaled, full


def on_device(tokens, expert_ids, gate_prob, w_gate, w_up, w_down, grad_out):
    tok_rows, fanout = expert_ids.shape
    per_device, width, hidden_units = w_gate.shape
    columns = lax.axis_size("expert")
    me = lax.axis_index("expert")
    capacity = 2 * tok_rows * fanout // (per_device * columns)
    dense = capacity >= tok_rows
    experts_all = per_device * columns
    picked = expert_ids[:, :, None] == jnp.arange(experts_all, dtype=jnp.int32)
    prob_of = jnp.sum(jnp.where(picked, gate_prob[:, :, None], 0.0), axis=1)
    pad = -3 * experts_all % 128
    packed = jnp.concatenate(
        [tokens, grad_out, *split_bf16(prob_of), jnp.zeros((tok_rows, pad), jnp.bfloat16)], axis=1
    )
    gathered = lax.all_gather(packed, "expert", axis=0, tiled=True)
    count = gathered.shape[0]
    x_all = gathered[:, :width]
    g_all = gathered[:, width : 2 * width]
    pieces = gathered[:, 2 * width : 2 * width + 3 * experts_all].astype(jnp.float32)
    pieces = pieces.reshape(count, 3, experts_all)
    prob_all = pieces[:, 0] + pieces[:, 1] + pieces[:, 2]
    prob_here = lax.dynamic_slice_in_dim(prob_all, me * per_device, per_device, 1).T
    if dense:
        x_rows, g_rows, probs = x_all[None], g_all[None], prob_here[:, :, None]
    else:
        blocks = prob_here.reshape(per_device, columns, tok_rows)
        chosen = (blocks > 0).astype(jnp.int32)
        rank = jnp.cumsum(chosen, axis=2) - 1
        slots = jnp.arange(capacity, dtype=jnp.int32)[:, None]
        hit = (rank[:, :, None, :] == slots) & (chosen[:, :, None, :] > 0)
        local = jnp.sum(jnp.where(hit, jnp.arange(tok_rows, dtype=jnp.int32), 0), axis=3)
        row_of = local + jnp.arange(columns, dtype=jnp.int32)[:, None] * tok_rows
        row_of = row_of.reshape(per_device, columns * capacity)
        x_rows, g_rows = x_all[row_of], g_all[row_of]
        probs = jnp.sum(jnp.where(hit, blocks[:, :, None, :], 0.0), axis=3)
        probs = probs.reshape(per_device, columns * capacity, 1)
    scaled, full = exchange(x_rows, g_rows, probs, w_gate, w_up, w_down)
    hidden = full[:, :, :hidden_units]
    gate_grad = full[:, :, hidden_units : 2 * hidden_units]
    up_grad = full[:, :, 2 * hidden_units :]

    def dot(spec, a, b):
        return jnp.einsum(spec, a, b, preferred_element_type=jnp.float32)

    out = dot("grf,gfd->grd", hidden, w_down).astype(jnp.bfloat16).astype(jnp.float32)
    back = (dot("grf,gdf->grd", gate_grad, w_gate) + dot("grf,gdf->grd", up_grad, w_up)).astype(
        jnp.bfloat16
    )
    dots = jnp.sum(out * g_rows.astype(jnp.float32), axis=2)
    if dense:
        mixed_part = jnp.sum(probs * out, axis=0)
        grad_part = jnp.sum(back.astype(jnp.float32), axis=0)
        dots_of = jnp.where(prob_here > 0, dots, 0.0)
    else:
        flat = row_of.reshape(-1)
        start = jnp.zeros((count, width), jnp.float32)
        mixed_part = start.at[flat].add((probs * out).reshape(-1, width))
        real = jnp.where(probs > 0, back.astype(jnp.float32), 0.0)
        grad_part = start.at[flat].add(real.reshape(-1, width))
        expert_at = jnp.arange(per_device, dtype=jnp.int32)[:, None]
        dots_of = jnp.zeros((per_device, count), jnp.float32).at[expert_at, row_of].add(
            jnp.where(probs[:, :, 0] > 0, dots, 0.0)
        )
    parts = jnp.concatenate([mixed_part, grad_part], axis=1).astype(jnp.bfloat16)
    summed = lax.psum_scatter(parts, "expert", scatter_dimension=0, tiled=True)
    mixed, grad_tokens = summed[:, :width], summed[:, width:]
    wide = jnp.zeros((count, experts_all), jnp.float32)
    wide = lax.dynamic_update_slice_in_dim(wide, dots_of.T, me * per_device, 1)
    wide = lax.psum_scatter(wide, "expert", scatter_dimension=0, tiled=True)
    grad_gate = lax.psum(
        jnp.sum(jnp.where(picked, wide[:, None, :], 0.0), axis=2), "dp"
    )
    x_b = jnp.broadcast_to(x_rows, (per_device,) + x_rows.shape[1:])
    grad_w_gate = dot("grd,grf->gdf", x_b, gate_grad).astype(jnp.bfloat16)
    grad_w_up = dot("grd,grf->gdf", x_b, up_grad).astype(jnp.bfloat16)
    grad_w_down = dot("grf,grd->gfd", hidden, scaled).astype(jnp.bfloat16)
    return (mixed, grad_tokens, grad_gate, grad_w_gate, grad_w_up, grad_w_down)


def solution(mesh):
    return jax.shard_map(
        on_device,
        mesh=mesh,
        in_specs=(
            P("expert", "dp"),
            P("expert", None),
            P("expert", None),
            P("expert", "dp", None),
            P("expert", "dp", None),
            P("expert", None, "dp"),
            P("expert", "dp"),
        ),
        out_specs=(
            P("expert", "dp"),
            P("expert", "dp"),
            P("expert", None),
            P("expert", "dp", None),
            P("expert", "dp", None),
            P("expert", None, "dp"),
        ),
        check_vma=False,
    )
```

```python
import jax
import jax.numpy as jnp
from jax import lax
from jax.sharding import PartitionSpec as P


def split_bf16(value):
    high = value.astype(jnp.bfloat16)
    rest = value - high.astype(jnp.float32)
    mid = rest.astype(jnp.bfloat16)
    low = (rest - mid.astype(jnp.float32)).astype(jnp.bfloat16)
    return high, mid, low


def gather_line(block, axis):
    count = lax.axis_size(axis)
    me = lax.axis_index(axis)
    up_pairs = [(i, i + 1) for i in range(count - 1)]
    down_pairs = [(i + 1, i) for i in range(count - 1)]
    from_low, from_high = [], []
    low = high = block
    for _ in range(count - 1):
        low = lax.ppermute(low, axis, up_pairs)
        high = lax.ppermute(high, axis, down_pairs)
        from_low.append(low)
        from_high.append(high)
    line = jnp.concatenate(from_low[::-1] + [block] + from_high, axis=0)
    rows = block.shape[0]
    return lax.dynamic_slice_in_dim(line, (count - 1 - me) * rows, count * rows, 0)


def exchange(x_rows, g_rows, probs, w_gate, w_up, w_down):
    per_device, rows, _ = probs.shape
    hidden_units = w_gate.shape[2]
    experts = range(per_device)
    scaled = (probs * g_rows.astype(jnp.float32)).astype(jnp.bfloat16)

    def dot(spec, a, b):
        return jnp.einsum(spec, a, b, preferred_element_type=jnp.float32).astype(jnp.bfloat16)

    x_all = jnp.broadcast_to(x_rows, (per_device,) + x_rows.shape[1:])
    part = jnp.concatenate(
        [
            dot("grd,gdf->grf", x_all, w_gate),
            dot("grd,gdf->grf", x_all, w_up),
            dot("grd,gfd->grf", scaled, w_down),
        ],
        axis=2,
    ).reshape(per_device * rows, 3 * hidden_units)
    share = lax.psum_scatter(part, "dp", scatter_dimension=0, tiled=True).astype(jnp.float32)
    gate, up, hgrad = jnp.split(share, 3, axis=1)
    sig = jax.nn.sigmoid(gate)
    act = jnp.concatenate(
        [gate * sig * up, hgrad * up * sig * (1.0 + gate * (1.0 - sig)), hgrad * gate * sig],
        axis=1,
    ).astype(jnp.bfloat16)
    full = lax.all_gather(act, "dp", axis=0, tiled=True).reshape(per_device, rows, 3 * hidden_units)
    return scaled, full


def on_device(tokens, expert_ids, gate_prob, w_gate, w_up, w_down, grad_out):
    tok_rows, fanout = expert_ids.shape
    per_device, width, hidden_units = w_gate.shape
    columns = lax.axis_size("expert")
    me = lax.axis_index("expert")
    capacity = 2 * tok_rows * fanout // (per_device * columns)
    dense = capacity >= tok_rows
    experts_all = per_device * columns
    picked = expert_ids[:, :, None] == jnp.arange(experts_all, dtype=jnp.int32)
    prob_of = jnp.sum(jnp.where(picked, gate_prob[:, :, None], 0.0), axis=1)
    pad = -3 * experts_all % 128
    packed = jnp.concatenate(
        [tokens, grad_out, *split_bf16(prob_of), jnp.zeros((tok_rows, pad), jnp.bfloat16)], axis=1
    )
    gathered = gather_line(packed, "expert")
    count = gathered.shape[0]
    x_all = gathered[:, :width]
    g_all = gathered[:, width : 2 * width]
    pieces = gathered[:, 2 * width : 2 * width + 3 * experts_all].astype(jnp.float32)
    pieces = pieces.reshape(count, 3, experts_all)
    prob_all = pieces[:, 0] + pieces[:, 1] + pieces[:, 2]
    prob_here = lax.dynamic_slice_in_dim(prob_all, me * per_device, per_device, 1).T
    if dense:
        x_rows, g_rows, probs = x_all[None], g_all[None], prob_here[:, :, None]
    else:
        blocks = prob_here.reshape(per_device, columns, tok_rows)
        chosen = (blocks > 0).astype(jnp.int32)
        rank = jnp.cumsum(chosen, axis=2) - 1
        slots = jnp.arange(capacity, dtype=jnp.int32)[:, None]
        hit = (rank[:, :, None, :] == slots) & (chosen[:, :, None, :] > 0)
        local = jnp.sum(jnp.where(hit, jnp.arange(tok_rows, dtype=jnp.int32), 0), axis=3)
        row_of = local + jnp.arange(columns, dtype=jnp.int32)[:, None] * tok_rows
        row_of = row_of.reshape(per_device, columns * capacity)
        x_rows, g_rows = x_all[row_of], g_all[row_of]
        probs = jnp.sum(jnp.where(hit, blocks[:, :, None, :], 0.0), axis=3)
        probs = probs.reshape(per_device, columns * capacity, 1)
    scaled, full = exchange(x_rows, g_rows, probs, w_gate, w_up, w_down)
    hidden = full[:, :, :hidden_units]
    gate_grad = full[:, :, hidden_units : 2 * hidden_units]
    up_grad = full[:, :, 2 * hidden_units :]

    def dot(spec, a, b):
        return jnp.einsum(spec, a, b, preferred_element_type=jnp.float32)

    out = dot("grf,gfd->grd", hidden, w_down).astype(jnp.bfloat16).astype(jnp.float32)
    back = (dot("grf,gdf->grd", gate_grad, w_gate) + dot("grf,gdf->grd", up_grad, w_up)).astype(
        jnp.bfloat16
    )
    dots = jnp.sum(out * g_rows.astype(jnp.float32), axis=2)
    if dense:
        mixed_part = jnp.sum(probs * out, axis=0)
        grad_part = jnp.sum(back.astype(jnp.float32), axis=0)
        dots_of = jnp.where(prob_here > 0, dots, 0.0)
    else:
        flat = row_of.reshape(-1)
        start = jnp.zeros((count, width), jnp.float32)
        mixed_part = start.at[flat].add((probs * out).reshape(-1, width))
        real = jnp.where(probs > 0, back.astype(jnp.float32), 0.0)
        grad_part = start.at[flat].add(real.reshape(-1, width))
        expert_at = jnp.arange(per_device, dtype=jnp.int32)[:, None]
        dots_of = jnp.zeros((per_device, count), jnp.float32).at[expert_at, row_of].add(
            jnp.where(probs[:, :, 0] > 0, dots, 0.0)
        )
    parts = jnp.concatenate([mixed_part, grad_part], axis=1).astype(jnp.bfloat16)
    summed = lax.psum_scatter(parts, "expert", scatter_dimension=0, tiled=True)
    mixed, grad_tokens = summed[:, :width], summed[:, width:]
    wide = jnp.zeros((count, experts_all), jnp.float32)
    wide = lax.dynamic_update_slice_in_dim(wide, dots_of.T, me * per_device, 1)
    wide = lax.psum_scatter(wide, "expert", scatter_dimension=0, tiled=True)
    grad_gate = lax.psum(
        jnp.sum(jnp.where(picked, wide[:, None, :], 0.0), axis=2), "dp"
    )
    x_b = jnp.broadcast_to(x_rows, (per_device,) + x_rows.shape[1:])
    grad_w_gate = dot("grd,grf->gdf", x_b, gate_grad).astype(jnp.bfloat16)
    grad_w_up = dot("grd,grf->gdf", x_b, up_grad).astype(jnp.bfloat16)
    grad_w_down = dot("grf,grd->gfd", hidden, scaled).astype(jnp.bfloat16)
    return (mixed, grad_tokens, grad_gate, grad_w_gate, grad_w_up, grad_w_down)


def solution(mesh):
    return jax.shard_map(
        on_device,
        mesh=mesh,
        in_specs=(
            P("expert", "dp"),
            P("expert", None),
            P("expert", None),
            P("expert", "dp", None),
            P("expert", "dp", None),
            P("expert", None, "dp"),
            P("expert", "dp"),
        ),
        out_specs=(
            P("expert", "dp"),
            P("expert", "dp"),
            P("expert", None),
            P("expert", "dp", None),
            P("expert", "dp", None),
            P("expert", None, "dp"),
        ),
        check_vma=False,
    )
```
